32 devices in a mesh: row: 4 (over y, core), col: 8 (over z, x).
Axes of the slice: x: 2, y: 2, z: 4, core: 2. Of those that a mesh axis runs over, the one named last changes fastest.
Arguments:
- fringes: bfloat16 [32768, 32768], P(('row', 'col')), may hold values from -24 to 24
- lobe_bounds: int32 [64, 2], replicated, may hold values from 0 to 4096, as said below
- zone_index: int32 [1024, 64], P(('row', 'col')), may hold values from 0 to 1023
- zone_table: float32 [4, 1024], P(None, ('row', 'col')), may hold values from -6 to 6
Outputs:
- heights: bfloat16 [16384, 32768], P(('row', 'col'))
The draws below stay inside these ranges and needn't reach their ends.
Inputs may be any that keep to these rules, and one draw needn't show every extreme that they name: For every band t, lobe_bounds[t, 0] < lobe_bounds[t, 1]; some band starts at 0 and some band ends at 4096.
All inputs are finite; a program needn't handle non-finite values.
Results may differ from the reference program's by a relative error of at most 0.023.
Values may be sent and summed in bfloat16 or wider, within the bound.
No kernel may reach another device: no remote copies, remote signals or barrier semaphores. Data moves between devices by JAX's collectives and lax.ppermute only.
A program may use at most 192 MiB of HBM per device.

```python
import math
import jax
import jax.numpy as jnp
from jax import lax

W = 32768
H = 32768
W1 = 128
H1 = 128
KY_TILES = 64
ZB_R = 16
ZB_C = 512
LOBE = 4096
LOBE_START = 4096
NZONES = 1024


def draw_lobe_bounds(key, part):
    lower_key, width_key, zero_key, full_key = jax.random.split(key, 4)
    lower_edge = jax.random.randint(lower_key, (KY_TILES,), 0, LOBE // 2, dtype=jnp.int32)
    widths = jax.random.randint(width_key, (KY_TILES,), LOBE // 4, LOBE // 2 + 1, dtype=jnp.int32)
    upper_edge = lower_edge + widths
    zero_tile = jax.random.randint(zero_key, (), 0, KY_TILES, dtype=jnp.int32)
    full_tile = (zero_tile + 1 + jax.random.randint(full_key, (), 0, KY_TILES - 1, dtype=jnp.int32)) % KY_TILES
    tile_index = jnp.arange(KY_TILES, dtype=jnp.int32)
    lower_edge = jnp.where(tile_index == zero_tile, 0, lower_edge)
    upper_edge = jnp.where(tile_index == full_tile, LOBE, upper_edge)
    return jnp.stack([lower_edge, upper_edge], axis=1).astype(jnp.int32)


def plant(drawn, rng, smallest, high):
    place = [jax.random.randint(jax.random.fold_in(rng, axis), (), 0, length) for axis, length in enumerate(drawn.shape)]
    main_axis = drawn.shape.index(max(drawn.shape))
    neighbour = place[:main_axis] + [(place[main_axis] + 1) % drawn.shape[main_axis]] + place[main_axis + 1:]
    return drawn.at[tuple(place)].set(smallest).at[tuple(neighbour)].set(high)


def level_of(stream_key, extent, cuts, smallest, top_value):
    def one(dim, blocks):
        steps = jax.random.uniform(jax.random.fold_in(jax.random.fold_in(stream_key, 6), dim), (blocks,), jnp.float32, smallest / len(cuts), top_value / len(cuts))
        return jnp.repeat(jnp.exp(steps), extent[dim] // blocks).reshape((-1,) + (1,) * (len(extent) - dim - 1))

    gain = one(*cuts[0])
    for cut in cuts[1:]:
        gain = gain * one(*cut)
    return gain


def centred(key, dims, width, reach, cuts=(), held_as=jnp.bfloat16):
    values = width * jax.random.normal(key, dims, jnp.float32)
    if cuts:
        values = values * level_of(key, dims, cuts, -0.22, 0.18)
    return jnp.clip(values, -reach, reach).astype(held_as)


def setup_inputs(seed: int = 0) -> dict:
    streams_of = jax.random.split(jax.random.key(seed), 5)
    fringes = centred(streams_of[0], (H, W), 4.0, 24.0, ((0, 32),))
    lobe_bounds = draw_lobe_bounds(jax.random.fold_in(streams_of[4], 71), 0)
    zone_index = plant(jax.random.randint(streams_of[2], (H // (2 * ZB_R), W // ZB_C), 0, NZONES), jax.random.fold_in(streams_of[2], 1), 0, NZONES - 1).astype(jnp.int32)
    zone_table = centred(streams_of[3], (4, NZONES), 1.0, 6.0, ((1, 32),), jnp.float32)
    return {"fringes": fringes, "lobe_bounds": lobe_bounds, "zone_index": zone_index, "zone_table": zone_table}


damping_floor = 0.5

def phase_pair(first_count, second_count, period, offset):
    first_index = jnp.arange(first_count, dtype=jnp.int32)[:, None]
    second_index = jnp.arange(second_count, dtype=jnp.int32)[None, :] + offset
    turn_count = first_index * second_index % period
    angles = turn_count.astype(jnp.float32) * (2.0 * math.pi / period)
    return (jnp.cos(angles), jnp.sin(angles))

def table_pair(first_count, second_count, period, offset):
    cosine, sine_part = phase_pair(first_count, second_count, period, offset)
    return (cosine.astype(jnp.bfloat16), sine_part.astype(jnp.bfloat16))

def complex_mix(pattern, real_part, imag_part, cosine, sine_part, direction):
    real_data = real_part.astype(jnp.float32)
    imag_data = imag_part.astype(jnp.float32)
    cos_data = cosine.astype(jnp.float32)
    sin_data = sine_part.astype(jnp.float32)
    real_cos = jnp.einsum(pattern, real_data, cos_data)
    imag_sin = jnp.einsum(pattern, imag_data, sin_data)
    imag_cos = jnp.einsum(pattern, imag_data, cos_data)
    real_sin = jnp.einsum(pattern, real_data, sin_data)
    return (real_cos - direction * imag_sin, imag_cos + direction * real_sin)

def apply_twist(real_part, imag_part, cosine, sine_part, direction):
    out_real = real_part * cosine - direction * (imag_part * sine_part)
    out_imag = imag_part * cosine + direction * (real_part * sine_part)
    return (out_real, out_imag)

def row_forward(rows_block):
    row_total = rows_block.shape[0]
    shaped = rows_block.reshape(row_total, W1, W // W1).astype(jnp.float32)
    cosine, sine_part = table_pair(W1, W1, W1, 0)
    first_real = jnp.einsum('rab,ak->rkb', shaped, cosine.astype(jnp.float32))
    first_imag = -jnp.einsum('rab,ak->rkb', shaped, sine_part.astype(jnp.float32))
    twist_real, twist_imag = phase_pair(W1, W // W1, W, 0)
    middle_real, middle_imag = apply_twist(first_real, first_imag, twist_real, twist_imag, -1.0)
    middle_real = middle_real.astype(jnp.bfloat16)
    middle_imag = middle_imag.astype(jnp.bfloat16)
    cosine, sine_part = table_pair(W // W1, LOBE // W1, W // W1, LOBE_START // W1)
    lobe_real, lobe_imag = complex_mix('rkb,bj->rjk', middle_real, middle_imag, cosine, sine_part, -1.0)
    return jnp.stack([lobe_real, lobe_imag]).reshape(2, row_total, LOBE).astype(jnp.bfloat16)

def column_pass(columns, column_index, lower_edge, upper_edge):
    col_total = columns.shape[1]
    second_len = H // H1
    shaped_real = columns[0].reshape(col_total, H1, second_len)
    shaped_imag = columns[1].reshape(col_total, H1, second_len)
    cosine, sine_part = table_pair(H1, H1, H1, 0)
    first_real, first_imag = complex_mix('cab,ak->ckb', shaped_real, shaped_imag, cosine, sine_part, -1.0)
    twist_real, twist_imag = phase_pair(H1, second_len, H, 0)
    middle_real, middle_imag = apply_twist(first_real, first_imag, twist_real, twist_imag, -1.0)
    middle_real = middle_real.astype(jnp.bfloat16)
    middle_imag = middle_imag.astype(jnp.bfloat16)
    cosine, sine_part = table_pair(second_len, second_len, second_len, 0)
    spectrum_real, spectrum_imag = complex_mix('ckb,bm->cmk', middle_real, middle_imag, cosine, sine_part, -1.0)
    spectrum_real = spectrum_real.reshape(col_total, H)
    spectrum_imag = spectrum_imag.reshape(col_total, H)
    lower_rows = jnp.repeat(lower_edge, H // KY_TILES)
    upper_rows = jnp.repeat(upper_edge, H // KY_TILES)
    keep_mask = (column_index[:, None] >= lower_rows[None, :]) & (column_index[:, None] < upper_rows[None, :])
    masked_real = jnp.where(keep_mask, spectrum_real, 0.0)
    masked_imag = jnp.where(keep_mask, spectrum_imag, 0.0)
    half_rows = H // 2
    fold_scale = 1.0 / (H * W)
    folded_real = ((masked_real[:, :half_rows] + masked_real[:, half_rows:]) * fold_scale).astype(jnp.bfloat16)
    folded_imag = ((masked_imag[:, :half_rows] + masked_imag[:, half_rows:]) * fold_scale).astype(jnp.bfloat16)
    fold_len = second_len // 2
    folded_real = folded_real.reshape(col_total, fold_len, H1)
    folded_imag = folded_imag.reshape(col_total, fold_len, H1)
    cosine, sine_part = table_pair(fold_len, fold_len, fold_len, 0)
    half_real, half_imag = complex_mix('cmk,mq->cqk', folded_real, folded_imag, cosine, sine_part, 1.0)
    twist_real, twist_imag = phase_pair(fold_len, H1, half_rows, 0)
    middle_real, middle_imag = apply_twist(half_real, half_imag, twist_real, twist_imag, 1.0)
    middle_real = middle_real.astype(jnp.bfloat16)
    middle_imag = middle_imag.astype(jnp.bfloat16)
    cosine, sine_part = table_pair(H1, H1, H1, 0)
    out_real, out_imag = complex_mix('cqk,kp->cpq', middle_real, middle_imag, cosine, sine_part, 1.0)
    return jnp.stack([out_real, out_imag]).reshape(2, col_total, half_rows).astype(jnp.bfloat16)

def height_map(field_real, field_imag, coefficients):
    magnitude = jnp.sqrt(field_real * field_real + field_imag * field_imag)
    sine_value = field_imag / jnp.maximum(magnitude, damping_floor)
    row_total = field_real.shape[0]
    sine_value = sine_value.reshape(row_total // ZB_R, ZB_R, W // ZB_C, ZB_C)
    expanded = coefficients[:, :, None, :, None]
    heights = expanded[0] + sine_value * (expanded[1] + sine_value * (expanded[2] + sine_value * expanded[3]))
    return heights.reshape(row_total, W).astype(jnp.bfloat16)

def row_inverse(field_rows, coefficients):
    row_total = field_rows.shape[1]
    shaped_real = field_rows[0].reshape(row_total, LOBE // W1, W1)
    shaped_imag = field_rows[1].reshape(row_total, LOBE // W1, W1)
    cosine, sine_part = table_pair(LOBE // W1, W // W1, W // W1, 0)
    pixel_real, pixel_imag = complex_mix('rjk,jq->rkq', shaped_real, shaped_imag, cosine, sine_part, 1.0)
    twist_real, twist_imag = phase_pair(W1, W // W1, W, 0)
    middle_real, middle_imag = apply_twist(pixel_real, pixel_imag, twist_real, twist_imag, 1.0)
    middle_real = middle_real.astype(jnp.bfloat16)
    middle_imag = middle_imag.astype(jnp.bfloat16)
    cosine, sine_part = table_pair(W1, W1, W1, 0)
    field_real, field_imag = complex_mix('rkq,kp->rpq', middle_real, middle_imag, cosine, sine_part, 1.0)
    return height_map(field_real.reshape(row_total, W), field_imag.reshape(row_total, W), coefficients)

def reference(fringes, lobe_bounds, zone_index, zone_table):
    row_block = min(256, H)
    lobe_blocks = lax.map(row_forward, fringes.reshape(H // row_block, row_block, W))
    lobe_cols = lobe_blocks.transpose(1, 3, 0, 2).reshape(2, LOBE, H)
    col_block = min(128, LOBE)
    col_groups = lobe_cols.reshape(2, LOBE // col_block, col_block, H).transpose(1, 0, 2, 3)
    index_groups = jnp.arange(LOBE, dtype=jnp.int32).reshape(LOBE // col_block, col_block)

    def column_group(pieces):
        return column_pass(pieces[0], pieces[1], lobe_bounds[:, 0], lobe_bounds[:, 1])
    field_groups = lax.map(column_group, (col_groups, index_groups))
    half_rows = H // 2
    field_rows = field_groups.transpose(1, 3, 0, 2).reshape(2, half_rows, LOBE)
    out_block = math.gcd(half_rows, 128 * ZB_R)
    row_groups = field_rows.reshape(2, half_rows // out_block, out_block, LOBE).transpose(1, 0, 2, 3)
    zone_groups = zone_index.reshape(half_rows // out_block, out_block // ZB_R, W // ZB_C)

    def height_group(pieces):
        coefficients = zone_table[:, pieces[1]]
        return row_inverse(pieces[0], coefficients)
    heights = lax.map(height_group, (row_groups, zone_groups))
    return heights.reshape(half_rows, W)
```

```python
import functools
import math

import jax
import jax.numpy as jnp
import ml_dtypes
import numpy as np
from jax import lax
from jax.experimental import pallas as pl
from jax.experimental.pallas import tpu as pltpu
from jax.sharding import Mesh
from jax.sharding import PartitionSpec as P

ZB_R = 16
LOBE = 4096
LOBE_START = 4096
DAMPING_FLOOR = 0.5

RADIX = 64
UNITS = RADIX // 2
GROUP = 16
HALVES = UNITS // GROUP
LANES = 128
ROW_PARTS = 4

f32 = jnp.float32
bf16 = jnp.bfloat16
VMEM_LIMIT = 58 * 1024 * 1024


def plus(x, y):
    if x is None:
        return y
    if y is None:
        return x
    return (x[0] + y[0], x[1] + y[1])


def minus(x, y):
    if y is None:
        return x
    if x is None:
        return (-y[0], -y[1])
    return (x[0] - y[0], x[1] - y[1])


def plus_i(x, y, sign):
    if y is None:
        return x
    if x is None:
        return (-y[1], y[0]) if sign > 0 else (y[1], -y[0])
    if sign > 0:
        return (x[0] - y[1], x[1] + y[0])
    return (x[0] + y[1], x[1] - y[0])


def turn(x, num, den):
    num %= den
    if x is None or num == 0:
        return x
    re, im = x
    if 4 * num == den:
        return (-im, re)
    if 2 * num == den:
        return (-re, -im)
    if 4 * num == 3 * den:
        return (im, -re)
    half = math.sqrt(0.5)
    if 8 * num == den:
        return ((re - im) * half, (re + im) * half)
    if 8 * num == 3 * den:
        return ((re + im) * -half, (re - im) * half)
    if 8 * num == 5 * den:
        return ((im - re) * half, (re + im) * -half)
    if 8 * num == 7 * den:
        return ((re + im) * half, (im - re) * half)
    c = math.cos(2 * math.pi * num / den)
    s = math.sin(2 * math.pi * num / den)
    return (re * c - im * s, im * c + re * s)


def complex_fft(xs, sign):
    n = len(xs)
    if n == 1:
        return list(xs)
    if n == 2:
        return [plus(xs[0], xs[1]), minus(xs[0], xs[1])]
    even = complex_fft(xs[0::2], sign)
    one = complex_fft(xs[1::4], sign)
    three = complex_fft(xs[3::4], sign)
    out = [None] * n
    for k in range(n // 4):
        t1 = turn(one[k], sign * k, n)
        t3 = turn(three[k], sign * 3 * k, n)
        total, diff = plus(t1, t3), minus(t1, t3)
        out[k] = plus(even[k], total)
        out[k + n // 2] = minus(even[k], total)
        out[k + n // 4] = plus_i(even[k + n // 4], diff, sign)
        out[k + 3 * n // 4] = plus_i(even[k + n // 4], diff, -sign)
    return out


def real_fft(xs):
    n = len(xs)
    if n == 1:
        return [(xs[0], None)]
    if n == 2:
        return [(xs[0] + xs[1], None), (xs[0] - xs[1], None)]
    even = real_fft(xs[0::2])
    one = real_fft(xs[1::4])
    three = real_fft(xs[3::4])
    out = [None] * (n // 2 + 1)
    total, diff = one[0][0] + three[0][0], one[0][0] - three[0][0]
    out[0] = (even[0][0] + total, None)
    out[n // 2] = (even[0][0] - total, None)
    out[n // 4] = (even[n // 4][0], -diff)
    for k in range(1, n // 8 + 1):
        if one[k][1] is None:
            c1, s1 = math.cos(2 * math.pi * k / n), math.sin(2 * math.pi * k / n)
            c3, s3 = math.cos(6 * math.pi * k / n), math.sin(6 * math.pi * k / n)
            t1 = (one[k][0] * c1, one[k][0] * -s1)
            t3 = (three[k][0] * c3, three[k][0] * -s3)
        else:
            t1 = turn(one[k], -k, n)
            t3 = turn(three[k], -3 * k, n)
        total, diff = plus(t1, t3), minus(t1, t3)
        low, high = even[k], even[n // 4 - k]
        if low[1] is None:
            out[k] = (low[0] + total[0], total[1])
            out[n // 2 - k] = (low[0] - total[0], total[1])
        else:
            out[k] = (low[0] + total[0], low[1] + total[1])
            out[n // 2 - k] = (low[0] - total[0], total[1] - low[1])
        if k != n // 4 - k:
            if high[1] is None:
                out[n // 4 + k] = (high[0] + diff[1], -diff[0])
                out[n // 4 - k] = (high[0] - diff[1], -diff[0])
            else:
                out[n // 4 + k] = (high[0] + diff[1], -(high[1] + diff[0]))
                out[n // 4 - k] = (high[0] - diff[1], high[1] - diff[0])
    return out


def cos_sin(turns, period):
    angles = (turns % period) * (2.0 * np.pi / period)
    return np.cos(angles), np.sin(angles)


def as_bf16(table):
    return table.astype(np.float32).astype(ml_dtypes.bfloat16)


def forward_tables(width):
    points = width // RADIX
    per_residue = LOBE // RADIX
    b = np.arange(points)[:, None]
    twist_cos, twist_sin = cos_sin(np.arange(UNITS)[:, None] * b.T, width)
    j = LOBE_START // RADIX + np.arange(per_residue)[None, :]
    c1, s1 = cos_sin(b * j, points)
    c2, s2 = cos_sin(b * (j + 1), points)
    mix = np.block([[c1, c2, -s1, -s2], [s1, -s2, c1, -c2]])
    c3, s3 = cos_sin(b * (2 * j + 1), 2 * points)
    zero = np.zeros_like(c1)
    mix_real = np.block([[c1, zero, -s1, zero], [zero, c3, zero, -s3]])
    return twist_cos.astype(np.float32), twist_sin.astype(np.float32), as_bf16(mix), as_bf16(mix_real)


def inverse_tables(width):
    points = width // RADIX
    per_residue = LOBE // RADIX
    q = np.arange(points)[None, :]
    twist_cos, twist_sin = cos_sin(np.arange(RADIX)[:, None] * q, width)
    c, s = cos_sin(np.arange(per_residue)[:, None] * q, points)
    zero = np.zeros_like(c)
    mix = np.block([[c, s, zero, zero], [zero, zero, c, s], [-s, c, zero, zero], [zero, zero, -s, c]])
    return twist_cos.astype(np.float32), twist_sin.astype(np.float32), as_bf16(mix)


def column_tables(rows):
    part = rows // ROW_PARTS
    b = np.arange(part)[None, :]
    m = np.arange(part)[:, None]
    forward = []
    for q in range(ROW_PARTS):
        c, s = cos_sin(b * (q + ROW_PARTS * m), rows)
        forward.append(np.concatenate([c, s], axis=1))
    out_row = np.arange(rows // 2)[:, None]
    order = (np.arange(ROW_PARTS)[:, None] + ROW_PARTS * np.arange(part // 2)[None, :]).reshape(1, -1)
    c, s = cos_sin(out_row * order, rows // 2)
    return as_bf16(np.stack(forward)), as_bf16(np.concatenate([c, s], axis=1))


def unit_columns(unit):
    lane = jnp.arange(LANES, dtype=jnp.int32)
    per_residue = LOBE // RADIX
    second = jnp.where(unit == 0, RADIX // 2, RADIX - unit)
    return RADIX * (lane % per_residue) + jnp.where(lane < per_residue, unit, second)


def launch(kernel, held, operands, in_specs, aliases=None, **options):
    count = len(held)
    return pl.pallas_call(
        lambda *refs: kernel(*refs[count:]),
        in_specs=[pl.BlockSpec(memory_space=pl.ANY)] * count + in_specs,
        input_output_aliases={count + k: v for k, v in (aliases or {}).items()},
        compiler_params=pltpu.CompilerParams(vmem_limit_bytes=VMEM_LIMIT),
        cost_estimate=pl.CostEstimate(flops=1, bytes_accessed=1, transcendentals=0),
        **options,
    )(*held, *operands)


def whole(array):
    return pl.BlockSpec(array.shape, lambda *_: (0,) * array.ndim)


def forward_kernel(x_ref, cos_ref, sin_ref, mix_ref, real_ref, *refs):
    outs, z_ref = refs[:HALVES], refs[HALVES]
    rows, width = x_ref.shape
    points = width // RADIX
    tiles = points // LANES

    def tile(i, carry):
        r = pl.multiple_of((i // tiles) * 16, 16)
        l = pl.multiple_of((i % tiles) * LANES, LANES)
        here = pl.ds(r, 16)
        xs = [x_ref[here, pl.ds(a * points + l, LANES)].astype(f32) for a in range(RADIX)]
        spectrum = real_fft(xs)
        z_ref[0, here, pl.ds(l, LANES)] = spectrum[0][0].astype(bf16)
        z_ref[0, here, pl.ds(points + l, LANES)] = spectrum[UNITS][0].astype(bf16)
        for k in range(1, UNITS):
            re, im = spectrum[k]
            c = cos_ref[k : k + 1, pl.ds(l, LANES)]
            s = sin_ref[k : k + 1, pl.ds(l, LANES)]
            z_ref[k, here, pl.ds(l, LANES)] = (re * c + im * s).astype(bf16)
            z_ref[k, here, pl.ds(points + l, LANES)] = (im * c - re * s).astype(bf16)
        return carry

    lax.fori_loop(0, rows // 16 * tiles, tile, 0)
    for h in range(HALVES):
        z = z_ref[h * GROUP : (h + 1) * GROUP].reshape(GROUP * rows, 2 * points)
        lobe = jnp.dot(z, mix_ref[...], preferred_element_type=f32)
        outs[h][...] = lobe.astype(bf16).reshape(GROUP, rows, 2 * LANES)
    outs[0][0] = jnp.dot(z_ref[0], real_ref[...], preferred_element_type=f32).astype(bf16)


def row_forward(fringes, part, late, *held):
    rows, width = fringes.shape
    part_rows = rows // ROW_PARTS
    block = min(32, part_rows)
    steps = part_rows // block
    tables = forward_tables(width)
    operands = [fringes, *[jnp.asarray(t) for t in tables], *late]
    count = len(operands) - len(late)
    return launch(
        lambda *refs: forward_kernel(*refs[:count], *refs[count + len(late) :]),
        held,
        operands,
        grid=(steps,),
        in_specs=[pl.BlockSpec((block, width), lambda i: (part * steps + i, 0))]
        + [whole(t) for t in tables]
        + [pl.BlockSpec(memory_space=pl.ANY) for _ in late],
        out_specs=[
            pl.BlockSpec((GROUP, block, 2 * LANES), lambda i: (0, i, 0)),
            pl.BlockSpec((GROUP, block, 2 * LANES), lambda i: (0, part * steps + i, 0)),
        ],
        out_shape=[
            jax.ShapeDtypeStruct((GROUP, part_rows, 2 * LANES), bf16),
            jax.ShapeDtypeStruct((GROUP, rows, 2 * LANES), bf16),
        ],
        aliases={count: 1} if late else {},
        scratch_shapes=[pltpu.VMEM((UNITS, block, 2 * width // RADIX), bf16)],
        name="row_forward",
    )


def first_kernel(devices, x_ref, cos_ref, sin_ref, o_ref):
    rows = x_ref.shape[1]

    def step(i, carry):
        here = pl.ds(pl.multiple_of(i * 16, 16), 16)
        cos_tab = cos_ref[here, :]
        sin_tab = sin_ref[here, :]

        def load(e):
            return (x_ref[e, here, :LANES].astype(f32), x_ref[e, here, LANES:].astype(f32))

        coarse = [complex_fft([load(rho * 4 + gamma) for rho in range(4)], -1) for gamma in range(4)]
        for q in range(4):
            fine = [turn(coarse[gamma][q], -gamma * q, devices) for gamma in range(4)]
            fine = complex_fft(fine + [None] * (devices // 4 - 4), -1)
            for p in range(devices // 4):
                u = q + 4 * p
                re, im = fine[p]
                c = cos_tab[:, u : u + 1]
                s = sin_tab[:, u : u + 1]
                o_ref[u, here, :LANES] = (re * c + im * s).astype(bf16)
                o_ref[u, here, LANES:] = (im * c - re * s).astype(bf16)
        return carry

    lax.fori_loop(0, rows // 16, step, 0)


def column_first(received, cos_tab, sin_tab, part, devices, *held):
    total = cos_tab.shape[0]
    rows = total // ROW_PARTS
    block = min(32, rows)
    steps = rows // block
    start = part * steps if received.shape[1] == total else 0
    table = pl.BlockSpec((block, devices), lambda i: (part * steps + i, 0))
    return launch(
        functools.partial(first_kernel, devices),
        held,
        [received, cos_tab, sin_tab],
        grid=(steps,),
        in_specs=[pl.BlockSpec((GROUP, block, 2 * LANES), lambda i: (0, start + i, 0)), table, table],
        out_specs=pl.BlockSpec((devices, block, 2 * LANES), lambda i: (0, i, 0)),
        out_shape=jax.ShapeDtypeStruct((devices, rows, 2 * LANES), bf16),
        name="column_first",
    )


def middle_kernel(*refs):
    parts, (forward_ref, inverse_ref, mask_ref, o_ref) = refs[:ROW_PARTS], refs[ROW_PARTS:]
    count = parts[0].shape[1]
    xs = [(ref[0, :, :LANES].astype(f32), ref[0, :, LANES:].astype(f32)) for ref in parts]
    mixed = complex_fft(xs, -1)
    folded_re, folded_im = [], []
    for q in range(ROW_PARTS):
        re, im = mixed[q][0].astype(bf16), mixed[q][1].astype(bf16)
        data = jnp.concatenate(
            [jnp.concatenate([re, im], axis=1), jnp.concatenate([im, -re], axis=1)], axis=0
        )
        spectrum = jnp.dot(forward_ref[q], data, preferred_element_type=f32) * mask_ref[...]
        folded = (spectrum[: count // 2] + spectrum[count // 2 :]).astype(bf16)
        folded_re.append(folded[:, :LANES])
        folded_im.append(folded[:, LANES:])
    re = jnp.concatenate(folded_re, axis=0)
    im = jnp.concatenate(folded_im, axis=0)
    data = jnp.concatenate(
        [jnp.concatenate([re, im], axis=1), jnp.concatenate([-im, re], axis=1)], axis=0
    )
    o_ref[0] = jnp.dot(inverse_ref[...], data, preferred_element_type=f32).astype(bf16)


def column_middle(parts, mask, *held):
    devices, part_rows, _ = parts[0].shape
    rows = part_rows * ROW_PARTS
    tables = column_tables(rows)
    piece = pl.BlockSpec((1, part_rows, 2 * LANES), lambda u: (u, 0, 0))
    return launch(
        middle_kernel,
        held,
        [*parts, *[jnp.asarray(t) for t in tables], mask],
        grid=(devices,),
        in_specs=[piece] * ROW_PARTS + [whole(t) for t in tables] + [whole(mask)],
        out_specs=pl.BlockSpec((1, rows // 2, 2 * LANES), lambda u: (u, 0, 0)),
        out_shape=jax.ShapeDtypeStruct((devices, rows // 2, 2 * LANES), bf16),
        name="column_middle",
    )


def last_kernel(devices, groups, group_ref, x_ref, cos_ref, sin_ref, *outs):
    rows = x_ref.shape[1]
    columns = devices // 4

    def step(i, carry):
        here = pl.ds(pl.multiple_of(i * 16, 16), 16)
        cos_tab = cos_ref[here, :]
        sin_tab = sin_ref[here, :]
        xs = []
        for u in range(devices):
            re = x_ref[u, here, :LANES].astype(f32)
            im = x_ref[u, here, LANES:].astype(f32)
            c = cos_tab[:, u : u + 1]
            s = sin_tab[:, u : u + 1]
            xs.append((re * c - im * s, im * c + re * s))
        ys = complex_fft(xs, 1)
        for delta in range(groups):
            carry_over = (group_ref[0] + delta) // groups
            for rho in range(4):
                for gamma in range(4):
                    re, im = ys[columns * rho + 4 * delta + gamma]
                    e = (rho + carry_over) % 4 * 4 + gamma if delta else rho * 4 + gamma
                    outs[delta][e, here, :LANES] = re.astype(bf16)
                    outs[delta][e, here, LANES:] = im.astype(bf16)
        return carry

    lax.fori_loop(0, rows // 16, step, 0)


def column_last(terms, cos_tab, sin_tab, group, part, groups, *held):
    devices, total, _ = terms.shape
    rows = total // ROW_PARTS
    block = min(32, rows)
    steps = rows // block
    table = pl.BlockSpec((block, devices), lambda i: (part * steps + i, 0))
    return launch(
        functools.partial(last_kernel, devices, groups),
        held,
        [group, terms, cos_tab, sin_tab],
        grid=(steps,),
        in_specs=[
            pl.BlockSpec(memory_space=pltpu.SMEM),
            pl.BlockSpec((devices, block, 2 * LANES), lambda i: (0, part * steps + i, 0)),
            table,
            table,
        ],
        out_specs=[pl.BlockSpec((GROUP, block, 2 * LANES), lambda i: (0, i, 0))] * groups,
        out_shape=[jax.ShapeDtypeStruct((GROUP, rows, 2 * LANES), bf16)] * groups,
        name="column_last",
    )


def sum_kernel(*refs):
    o_ref = refs[-1]
    count = len(refs) // HALVES
    for h in range(HALVES):
        total = refs[h * count][...].astype(f32)
        for ref in refs[h * count + 1 : (h + 1) * count]:
            total = total + ref[...].astype(f32)
        o_ref[:, h] = total.astype(bf16)


def add(pieces, *held):
    operands = [piece for shares in pieces for piece in shares]
    members, rows, lanes = operands[0].shape
    block = 4
    return launch(
        sum_kernel,
        held,
        operands,
        grid=(members // block,),
        in_specs=[pl.BlockSpec((block, rows, lanes), lambda i: (i, 0, 0))] * len(operands),
        out_specs=pl.BlockSpec((block, HALVES, rows, lanes), lambda i: (i, 0, 0, 0)),
        out_shape=jax.ShapeDtypeStruct((members, HALVES, rows, lanes), bf16),
        name="sum_shares",
    )


def inverse_kernel(first_block, per_device, zone_ref, table_ref, field_ref, *refs):
    cos_ref, sin_ref, mix_ref = refs[:3]
    o_ref, token_ref, g_ref = refs[-3:]
    token_ref[...] = jnp.zeros_like(token_ref)
    rows, width = o_ref.shape
    points = width // RADIX
    block = first_block + pl.program_id(0)
    field = field_ref[...].reshape(UNITS * rows, 2 * LANES)
    g_ref[...] = jnp.dot(field, mix_ref[...], preferred_element_type=f32).reshape(
        UNITS, rows, 4 * points
    )

    def tile(i, carry):
        l = pl.multiple_of(i * LANES, LANES)

        def load(residue):
            if residue in (0, UNITS):
                unit, second = 0, residue != 0
            else:
                unit, second = (residue, False) if residue < UNITS else (RADIX - residue, True)
            unit = unit % GROUP * HALVES + unit // GROUP
            start = 2 * points if second else 0
            re = g_ref[unit, :, pl.ds(start + l, LANES)]
            im = g_ref[unit, :, pl.ds(start + points + l, LANES)]
            if residue == 0:
                return (re, im)
            c = cos_ref[residue : residue + 1, pl.ds(l, LANES)]
            s = sin_ref[residue : residue + 1, pl.ds(l, LANES)]
            return (re * c - im * s, im * c + re * s)

        pixels = complex_fft([load(residue) for residue in range(RADIX)], 1)
        for p in range(RADIX):
            re, im = pixels[p]
            power = jnp.maximum(re * re + im * im, DAMPING_FLOOR * DAMPING_FLOOR)
            sine = im * lax.rsqrt(power)
            zone = zone_ref[block * RADIX + p]
            base = zone // per_device * (4 * per_device) + zone % per_device
            e = [table_ref[base + r * per_device] for r in range(4)]
            height = e[0] + sine * (e[1] + sine * (e[2] + sine * e[3]))
            o_ref[:, pl.ds(p * points + l, LANES)] = height.astype(bf16)
        return carry

    lax.fori_loop(0, points // LANES, tile, 0)


def row_inverse(field, zones, table, previous, part, shape, per_device, *held):
    part_rows = field.shape[2]
    rows, width = shape
    steps = part_rows // ZB_R
    tables = inverse_tables(width)
    smem = pl.BlockSpec(memory_space=pltpu.SMEM)
    extra = [] if previous is None else [previous]
    operands = [zones, table, field, *[jnp.asarray(t) for t in tables], *extra]
    return launch(
        functools.partial(inverse_kernel, part * steps, per_device),
        held,
        operands,
        grid=(steps,),
        in_specs=[smem, smem]
        + [pl.BlockSpec((GROUP, HALVES, ZB_R, 2 * LANES), lambda i: (0, 0, i, 0))]
        + [whole(t) for t in tables]
        + [pl.BlockSpec(memory_space=pl.ANY) for _ in extra],
        out_specs=[
            pl.BlockSpec((ZB_R, width), lambda i: (part * steps + i, 0)),
            pl.BlockSpec((8, LANES), lambda i: (0, 0)),
        ],
        out_shape=[jax.ShapeDtypeStruct(shape, bf16), jax.ShapeDtypeStruct((8, LANES), f32)],
        scratch_shapes=[pltpu.VMEM((UNITS, ZB_R, 4 * width // RADIX), f32)],
        aliases={len(operands) - 1: 0} if extra else {},
        name="row_inverse",
    )


def phase_table(rows, devices, offset, period):
    row = jnp.arange(rows, dtype=jnp.int32)[:, None] + offset
    turns = row * jnp.arange(devices, dtype=jnp.int32)[None, :] % period
    angles = turns.astype(f32) * (2.0 * math.pi / period)
    return jnp.cos(angles), jnp.sin(angles)


def body(groups, fringes, lobe_bounds, zone_index, zone_table):
    rows, width = fringes.shape
    devices = groups * GROUP
    height = rows * devices
    every = ("row", "group", "member")
    inside = ("row", "member")
    group = lax.axis_index("group")
    member = lax.axis_index(inside)

    def exchange(block):
        return lax.all_to_all(block, inside, split_axis=0, concat_axis=0, tiled=True)

    per_device = zone_table.shape[1]
    spread = jnp.broadcast_to(zone_table[None], (devices, 4, per_device))
    table = lax.all_to_all(spread, every, split_axis=0, concat_axis=0, tiled=True).reshape(-1)
    zones = zone_index.reshape(-1)

    first_offset = 4 * group * rows
    forward_phase = phase_table(rows, devices, first_offset, height)
    inverse_phase = phase_table(rows // 2, devices, first_offset // 2, height // 2)

    part_list = range(ROW_PARTS)
    masks = []
    for h in range(HALVES):
        columns = unit_columns(member + h * GROUP)
        keep = (columns[None, :] >= lobe_bounds[:, :1]) & (columns[None, :] < lobe_bounds[:, 1:])
        keep = keep.astype(f32) * (1.0 / (height * width))
        masks.append(jnp.repeat(jnp.tile(keep, (1, 2)), rows // ROW_PARTS // keep.shape[0], axis=0))

    lobes, late, arrived = [], [], []
    for part in part_list:
        held = [lobes[-1]] if part >= 1 else []
        if part >= 2:
            held.append(arrived[part - 2])
        lobe, *late = row_forward(fringes, part, late, *held)
        lobes.append(lobe)
        arrived.append(exchange(lobe))
    arrived_late = exchange(late[0])
    firsts = [[], []]
    last = lobes[-1]
    for part in part_list:
        last = column_first(arrived[part], *forward_phase, part, devices, last)
        firsts[0].append(last)
    terms = [column_middle(firsts[0], masks[0])]

    def send(pieces):
        return [
            lax.ppermute(pieces[d], "group", [(g, (g + d) % groups) for g in range(groups)])
            for d in range(1, groups)
        ]

    shares = []

    def finish(index, before):
        h, part = index // ROW_PARTS, index % ROW_PARTS
        held = [before] + (shares[index - 2][1:] if index >= 2 else [])
        pieces = column_last(terms[h], *inverse_phase, group.reshape(1), part, groups, *held)
        shares.append([pieces[0], *send(pieces)])
        return pieces[0]

    last = terms[0]
    for part in part_list:
        last = finish(part, last)
        if part % 2 == 1:
            for other in (part - 1, part):
                last = column_first(arrived_late, *forward_phase, other, devices, last)
                firsts[1].append(last)
    terms.append(column_middle(firsts[1], masks[1], last))
    last = terms[1]
    fields, result, token = [], None, None

    def gather(part, before):
        total = add([shares[part], shares[ROW_PARTS + part]], before)
        fields.append(exchange(total))
        return total

    for part in part_list:
        last = finish(ROW_PARTS + part, last)
        if part >= 2:
            last = gather(part - 2, last)
    for part in part_list:
        result, token = row_inverse(
            fields[part], zones, table, result, part, (rows // 2, width), per_device, last
        )
        last = token
        if part + 2 < ROW_PARTS:
            last = gather(part + 2, last)
    return result


def solution(mesh):
    row_size, col_size = mesh.shape["row"], mesh.shape["col"]
    groups = row_size * col_size // GROUP
    split = Mesh(
        mesh.devices.reshape(row_size, groups, col_size // groups), ("row", "group", "member")
    )
    every = ("row", "group", "member")
    placed = (P(every, None), P(), P(every, None), P(None, every))
    return jax.shard_map(
        functools.partial(body, groups),
        mesh=split,
        in_specs=placed,
        out_specs=P(every, None),
        check_vma=False,
    )
```

```python
import functools
import math

import jax
import jax.numpy as jnp
import ml_dtypes
import numpy as np
from jax import lax
from jax.experimental import pallas as pl
from jax.experimental.pallas import tpu as pltpu
from jax.sharding import Mesh
from jax.sharding import PartitionSpec as P

ZB_R = 16
LOBE = 4096
LOBE_START = 4096
DAMPING_FLOOR = 0.5

RADIX = 64
UNITS = RADIX // 2
GROUP = 16
HALVES = UNITS // GROUP
LANES = 128
ROW_PARTS = 4
OUT_PARTS = (2, 2, 2, 2)

f32 = jnp.float32
bf16 = jnp.bfloat16
VMEM_LIMIT = 58 * 1024 * 1024


def plus(x, y):
    if x is None:
        return y
    if y is None:
        return x
    return (x[0] + y[0], x[1] + y[1])


def minus(x, y):
    if y is None:
        return x
    if x is None:
        return (-y[0], -y[1])
    return (x[0] - y[0], x[1] - y[1])


def plus_i(x, y, sign):
    if y is None:
        return x
    if x is None:
        return (-y[1], y[0]) if sign > 0 else (y[1], -y[0])
    if sign > 0:
        return (x[0] - y[1], x[1] + y[0])
    return (x[0] + y[1], x[1] - y[0])


def turn(x, num, den):
    num %= den
    if x is None or num == 0:
        return x
    re, im = x
    if 4 * num == den:
        return (-im, re)
    if 2 * num == den:
        return (-re, -im)
    if 4 * num == 3 * den:
        return (im, -re)
    half = math.sqrt(0.5)
    if 8 * num == den:
        return ((re - im) * half, (re + im) * half)
    if 8 * num == 3 * den:
        return ((re + im) * -half, (re - im) * half)
    if 8 * num == 5 * den:
        return ((im - re) * half, (re + im) * -half)
    if 8 * num == 7 * den:
        return ((re + im) * half, (im - re) * half)
    c = math.cos(2 * math.pi * num / den)
    s = math.sin(2 * math.pi * num / den)
    return (re * c - im * s, im * c + re * s)


def complex_fft(xs, sign):
    n = len(xs)
    if n == 1:
        return list(xs)
    if n == 2:
        return [plus(xs[0], xs[1]), minus(xs[0], xs[1])]
    even = complex_fft(xs[0::2], sign)
    one = complex_fft(xs[1::4], sign)
    three = complex_fft(xs[3::4], sign)
    out = [None] * n
    for k in range(n // 4):
        t1 = turn(one[k], sign * k, n)
        t3 = turn(three[k], sign * 3 * k, n)
        total, diff = plus(t1, t3), minus(t1, t3)
        out[k] = plus(even[k], total)
        out[k + n // 2] = minus(even[k], total)
        out[k + n // 4] = plus_i(even[k + n // 4], diff, sign)
        out[k + 3 * n // 4] = plus_i(even[k + n // 4], diff, -sign)
    return out


def real_fft(xs):
    n = len(xs)
    if n == 1:
        return [(xs[0], None)]
    if n == 2:
        return [(xs[0] + xs[1], None), (xs[0] - xs[1], None)]
    even = real_fft(xs[0::2])
    one = real_fft(xs[1::4])
    three = real_fft(xs[3::4])
    out = [None] * (n // 2 + 1)
    total, diff = one[0][0] + three[0][0], one[0][0] - three[0][0]
    out[0] = (even[0][0] + total, None)
    out[n // 2] = (even[0][0] - total, None)
    out[n // 4] = (even[n // 4][0], -diff)
    for k in range(1, n // 8 + 1):
        if one[k][1] is None:
            c1, s1 = math.cos(2 * math.pi * k / n), math.sin(2 * math.pi * k / n)
            c3, s3 = math.cos(6 * math.pi * k / n), math.sin(6 * math.pi * k / n)
            t1 = (one[k][0] * c1, one[k][0] * -s1)
            t3 = (three[k][0] * c3, three[k][0] * -s3)
        else:
            t1 = turn(one[k], -k, n)
            t3 = turn(three[k], -3 * k, n)
        total, diff = plus(t1, t3), minus(t1, t3)
        low, high = even[k], even[n // 4 - k]
        if low[1] is None:
            out[k] = (low[0] + total[0], total[1])
            out[n // 2 - k] = (low[0] - total[0], total[1])
        else:
            out[k] = (low[0] + total[0], low[1] + total[1])
            out[n // 2 - k] = (low[0] - total[0], total[1] - low[1])
        if k != n // 4 - k:
            if high[1] is None:
                out[n // 4 + k] = (high[0] + diff[1], -diff[0])
                out[n // 4 - k] = (high[0] - diff[1], -diff[0])
            else:
                out[n // 4 + k] = (high[0] + diff[1], -(high[1] + diff[0]))
                out[n // 4 - k] = (high[0] - diff[1], high[1] - diff[0])
    return out


def cos_sin(turns, period):
    angles = (turns % period) * (2.0 * np.pi / period)
    return np.cos(angles), np.sin(angles)


def as_bf16(table):
    return table.astype(np.float32).astype(ml_dtypes.bfloat16)


def forward_tables(width):
    points = width // RADIX
    per_residue = LOBE // RADIX
    b = np.arange(points)[:, None]
    twist_cos, twist_sin = cos_sin(np.arange(UNITS + 1)[:, None] * b.T, width)
    j = LOBE_START // RADIX + np.arange(per_residue)[None, :]
    c1, s1 = cos_sin(b * j, points)
    c2, s2 = cos_sin(b * (j + 1), points)
    mix = np.block([[c1, c2, -s1, -s2], [s1, -s2, c1, -c2]])
    return twist_cos.astype(np.float32), twist_sin.astype(np.float32), as_bf16(mix)


def inverse_tables(width):
    points = width // RADIX
    per_residue = LOBE // RADIX
    q = np.arange(points)[None, :]
    residue = np.arange(UNITS)[:, None]
    turns = np.concatenate([residue * q, residue * (q + points)])
    twist_cos, twist_sin = cos_sin(turns, width)
    column = np.arange(per_residue)[:, None]
    c1, s1 = cos_sin(column * q, points)
    c2, s2 = cos_sin((2 * column + 1) * q, 2 * points)
    mix = np.block([[c1, s1, c1, s1], [c2, s2, -c2, -s2], [-s1, c1, -s1, c1], [-s2, c2, s2, -c2]])
    return twist_cos.astype(np.float32), twist_sin.astype(np.float32), as_bf16(mix)


def column_tables(rows):
    part = rows // ROW_PARTS
    b = np.arange(part)[None, :]
    m = np.arange(part)[:, None]
    forward = []
    for q in range(ROW_PARTS):
        c, s = cos_sin(b * (q + ROW_PARTS * m), rows)
        forward.append(np.concatenate([c, s], axis=1))
    out_row = np.arange(rows // 2)[:, None]
    order = (np.arange(ROW_PARTS)[:, None] + ROW_PARTS * np.arange(part // 2)[None, :]).reshape(1, -1)
    c, s = cos_sin(out_row * order, rows // 2)
    return as_bf16(np.stack(forward)), as_bf16(np.concatenate([c, s], axis=1))


def out_part(part, rows):
    eighth = rows // 8
    return sum(OUT_PARTS[:part]) * eighth, OUT_PARTS[part] * eighth


def unit_columns(unit):
    lane = jnp.arange(LANES, dtype=jnp.int32)
    per_residue = LOBE // RADIX
    second = jnp.where(unit == 0, RADIX // 2, RADIX - unit)
    return RADIX * (lane % per_residue) + jnp.where(lane < per_residue, unit, second)


def launch(kernel, held, operands, in_specs, aliases=None, cost=1, **options):
    count = len(held)
    return pl.pallas_call(
        lambda *refs: kernel(*refs[count:]),
        in_specs=[pl.BlockSpec(memory_space=pl.ANY)] * count + in_specs,
        input_output_aliases={count + k: v for k, v in (aliases or {}).items()},
        compiler_params=pltpu.CompilerParams(vmem_limit_bytes=VMEM_LIMIT),
        cost_estimate=pl.CostEstimate(flops=cost, bytes_accessed=cost, transcendentals=0),
        **options,
    )(*held, *operands)


def gate(value, *held):
    spec = pl.BlockSpec(memory_space=pl.ANY)
    return launch(
        lambda *refs: None,
        held,
        [value],
        in_specs=[spec],
        out_specs=spec,
        out_shape=jax.ShapeDtypeStruct(value.shape, value.dtype),
        aliases={0: 0},
        name="gate",
    )


def whole(array):
    return pl.BlockSpec(array.shape, lambda *_: (0,) * array.ndim)


def forward_kernel(x_ref, cos_ref, sin_ref, mix_ref, *refs):
    outs, slots = refs[:HALVES], refs[HALVES:]
    rows, width = x_ref.shape
    points = width // RADIX
    tiles = points // LANES
    lane = lax.broadcasted_iota(jnp.int32, (16, 2 * LANES), 1)
    first_residue = lane % LANES < LANES // 2

    def butterfly(z_ref, r, l):
        here = pl.ds(r, 16)
        xs = [x_ref[here, pl.ds(a * points + l, LANES)].astype(f32) for a in range(RADIX)]
        spectrum = real_fft(xs)
        z_ref[0, :, pl.ds(l, LANES)] = spectrum[0][0].astype(bf16)
        z_ref[0, :, pl.ds(points + l, LANES)] = jnp.zeros((16, LANES), bf16)
        for k in range(1, UNITS + 1):
            re, im = spectrum[k]
            c = cos_ref[k : k + 1, pl.ds(l, LANES)]
            s = sin_ref[k : k + 1, pl.ds(l, LANES)]
            if im is None:
                z_ref[k, :, pl.ds(l, LANES)] = (re * c).astype(bf16)
                z_ref[k, :, pl.ds(points + l, LANES)] = (re * -s).astype(bf16)
            else:
                z_ref[k, :, pl.ds(l, LANES)] = (re * c + im * s).astype(bf16)
                z_ref[k, :, pl.ds(points + l, LANES)] = (im * c - re * s).astype(bf16)

    def mix(z_ref, r):
        z = z_ref[...].reshape((UNITS + 1) * 16, 2 * points)
        lobe = jnp.dot(z, mix_ref[...], preferred_element_type=f32)
        lobe = lobe.astype(bf16).reshape(UNITS + 1, 16, 2 * LANES)
        here = pl.ds(r, 16)
        outs[0][0, here] = jnp.where(first_residue, lobe[0], lobe[UNITS])
        outs[0][1:, here] = lobe[1:GROUP]
        for h in range(1, HALVES):
            outs[h][:, here] = lobe[h * GROUP : (h + 1) * GROUP]

    for g in range(rows // 16):
        for t in range(tiles):
            butterfly(slots[0], g * 16, t * LANES)
        mix(slots[0], g * 16)


def row_forward(fringes, part, late, *held):
    rows, width = fringes.shape
    part_rows = rows // ROW_PARTS
    block = min(16, part_rows)
    steps = part_rows // block
    tables = forward_tables(width)
    operands = [fringes, *[jnp.asarray(t) for t in tables], *late]
    count = len(operands) - len(late)
    return launch(
        lambda *refs: forward_kernel(*refs[:count], *refs[count + len(late) :]),
        held,
        operands,
        grid=(steps,),
        in_specs=[pl.BlockSpec((block, width), lambda i: (part * steps + i, 0))]
        + [whole(t) for t in tables]
        + [pl.BlockSpec(memory_space=pl.ANY) for _ in late],
        out_specs=[
            pl.BlockSpec((GROUP, block, 2 * LANES), lambda i: (0, i, 0)),
            pl.BlockSpec((GROUP, block, 2 * LANES), lambda i: (0, part * steps + i, 0)),
        ],
        out_shape=[
            jax.ShapeDtypeStruct((GROUP, part_rows, 2 * LANES), bf16),
            jax.ShapeDtypeStruct((GROUP, rows, 2 * LANES), bf16),
        ],
        aliases={count: 1} if late else {},
        scratch_shapes=[pltpu.VMEM((UNITS + 1, 16, 2 * width // RADIX), bf16)] * 2,
        name="row_forward",
    )


def first_kernel(devices, x_ref, cos_ref, sin_ref, o_ref):
    rows = x_ref.shape[1]

    def step(i, carry):
        here = pl.ds(pl.multiple_of(i * 16, 16), 16)
        cos_tab = cos_ref[here, :]
        sin_tab = sin_ref[here, :]

        def load(e):
            return (x_ref[e, here, :LANES].astype(f32), x_ref[e, here, LANES:].astype(f32))

        coarse = [complex_fft([load(rho * 4 + gamma) for rho in range(4)], -1) for gamma in range(4)]
        for q in range(4):
            fine = [turn(coarse[gamma][q], -gamma * q, devices) for gamma in range(4)]
            fine = complex_fft(fine + [None] * (devices // 4 - 4), -1)
            for p in range(devices // 4):
                u = q + 4 * p
                re, im = fine[p]
                c = cos_tab[:, u : u + 1]
                s = sin_tab[:, u : u + 1]
                o_ref[u, here, :LANES] = (re * c + im * s).astype(bf16)
                o_ref[u, here, LANES:] = (im * c - re * s).astype(bf16)
        return carry

    lax.fori_loop(0, rows // 16, step, 0)


def column_first(received, cos_tab, sin_tab, part, devices, *held):
    total, rows = cos_tab.shape[0], received.shape[1]
    block = min(64, total // ROW_PARTS)
    steps = rows // block
    start = 0 if rows == total else part * steps
    table = pl.BlockSpec((block, devices), lambda i: (start + i, 0))
    return launch(
        functools.partial(first_kernel, devices),
        held,
        [received, cos_tab, sin_tab],
        grid=(steps,),
        in_specs=[pl.BlockSpec((GROUP, block, 2 * LANES), lambda i: (0, i, 0)), table, table],
        out_specs=pl.BlockSpec((devices, block, 2 * LANES), lambda i: (0, i, 0)),
        out_shape=jax.ShapeDtypeStruct((devices, rows, 2 * LANES), bf16),
        name="column_first",
    )


def middle_kernel(*refs):
    parts, (forward_ref, inverse_ref, mask_ref, o_ref) = refs[:ROW_PARTS], refs[ROW_PARTS:]
    count = parts[0].shape[1]
    for u in range(o_ref.shape[0]):
        xs = [(ref[u, :, :LANES].astype(f32), ref[u, :, LANES:].astype(f32)) for ref in parts]
        mixed = complex_fft(xs, -1)
        folded_re, folded_im = [], []
        for q in range(ROW_PARTS):
            re, im = mixed[q][0].astype(bf16), mixed[q][1].astype(bf16)
            data = jnp.concatenate(
                [jnp.concatenate([re, im], axis=1), jnp.concatenate([im, -re], axis=1)], axis=0
            )
            spectrum = jnp.dot(forward_ref[q], data, preferred_element_type=f32) * mask_ref[...]
            folded = (spectrum[: count // 2] + spectrum[count // 2 :]).astype(bf16)
            folded_re.append(folded[:, :LANES])
            folded_im.append(folded[:, LANES:])
        re = jnp.concatenate(folded_re, axis=0)
        im = jnp.concatenate(folded_im, axis=0)
        data = jnp.concatenate(
            [jnp.concatenate([re, im], axis=1), jnp.concatenate([-im, re], axis=1)], axis=0
        )
        o_ref[u] = jnp.dot(inverse_ref[...], data, preferred_element_type=f32).astype(bf16)


def column_middle(parts, mask, *held):
    devices = parts[0].shape[0]
    rows = sum(part.shape[1] for part in parts)
    part_rows = rows // ROW_PARTS
    block = 4
    tables = column_tables(rows)
    if len(parts) == 1:
        parts = parts * ROW_PARTS
        places = range(ROW_PARTS)
    else:
        places = [0] * ROW_PARTS
    pieces = [pl.BlockSpec((block, part_rows, 2 * LANES), lambda u, r=r: (u, r, 0)) for r in places]
    return launch(
        middle_kernel,
        held,
        [*parts, *[jnp.asarray(t) for t in tables], mask],
        grid=(devices // block,),
        in_specs=pieces + [whole(t) for t in tables] + [whole(mask)],
        out_specs=pl.BlockSpec((block, rows // 2, 2 * LANES), lambda u: (u, 0, 0)),
        out_shape=jax.ShapeDtypeStruct((devices, rows // 2, 2 * LANES), bf16),
        name="column_middle",
    )


def last_kernel(devices, groups, group_ref, x_ref, cos_ref, sin_ref, *outs):
    rows = x_ref.shape[1]
    columns = devices // 4

    def step(i, carry):
        here = pl.ds(pl.multiple_of(i * 16, 16), 16)
        cos_tab = cos_ref[here, :]
        sin_tab = sin_ref[here, :]
        xs = []
        for u in range(devices):
            re = x_ref[u, here, :LANES].astype(f32)
            im = x_ref[u, here, LANES:].astype(f32)
            c = cos_tab[:, u : u + 1]
            s = sin_tab[:, u : u + 1]
            xs.append((re * c - im * s, im * c + re * s))
        ys = complex_fft(xs, 1)
        for delta in range(groups):
            carry_over = (group_ref[0] + delta) // groups
            for rho in range(4):
                for gamma in range(4):
                    re, im = ys[columns * rho + 4 * delta + gamma]
                    e = (rho + carry_over) % 4 * 4 + gamma if delta else rho * 4 + gamma
                    outs[delta][e, here, :LANES] = re.astype(bf16)
                    outs[delta][e, here, LANES:] = im.astype(bf16)
        return carry

    lax.fori_loop(0, rows // 16, step, 0)


def column_last(terms, cos_tab, sin_tab, group, part, groups, *held):
    devices, total, _ = terms.shape
    first, rows = out_part(part, total)
    block = min(64, rows)
    steps = rows // block
    start = first // block
    table = pl.BlockSpec((block, devices), lambda i: (start + i, 0))
    return launch(
        functools.partial(last_kernel, devices, groups),
        held,
        [group, terms, cos_tab, sin_tab],
        grid=(steps,),
        in_specs=[
            pl.BlockSpec(memory_space=pltpu.SMEM),
            pl.BlockSpec((devices, block, 2 * LANES), lambda i: (0, start + i, 0)),
            table,
            table,
        ],
        out_specs=[pl.BlockSpec((GROUP, block, 2 * LANES), lambda i: (0, i, 0))] * groups,
        out_shape=[jax.ShapeDtypeStruct((GROUP, rows, 2 * LANES), bf16)] * groups,
        name="column_last",
    )


def sum_kernel(*refs):
    o_ref = refs[-1]
    count = len(refs) // HALVES
    for h in range(HALVES):
        total = refs[h * count][...].astype(f32)
        for ref in refs[h * count + 1 : (h + 1) * count]:
            total = total + ref[...].astype(f32)
        o_ref[:, h] = total.astype(bf16)


def add(pieces, *held):
    operands = [piece for shares in pieces for piece in shares]
    members, rows, lanes = operands[0].shape
    block = 4
    return launch(
        sum_kernel,
        held,
        operands,
        grid=(members // block,),
        in_specs=[pl.BlockSpec((block, rows, lanes), lambda i: (i, 0, 0))] * len(operands),
        out_specs=pl.BlockSpec((block, HALVES, rows, lanes), lambda i: (i, 0, 0, 0)),
        out_shape=jax.ShapeDtypeStruct((members, HALVES, rows, lanes), bf16),
        name="sum_shares",
    )


def inverse_kernel(first_block, per_device, zone_ref, table_ref, field_ref, *refs):
    cos_ref, sin_ref, mix_ref = refs[:3]
    o_ref, token_ref, f_ref, g_ref, e_ref = refs[-5:]
    token_ref[...] = jnp.zeros_like(token_ref)
    rows, width = o_ref.shape
    points = width // RADIX
    blocks = rows // ZB_R
    block = first_block + pl.program_id(0) * blocks
    lane = lax.broadcasted_iota(jnp.int32, (rows, 2 * LANES), 1)
    first_residue = lane % LANES < LANES // 2

    def unit(u):
        return field_ref[u % GROUP, u // GROUP]

    for k in range(UNITS):
        f_ref[k] = jnp.where(first_residue, unit(k), unit(-k % UNITS))
    g_ref[...] = jnp.dot(
        f_ref[...].reshape(UNITS * rows, 2 * LANES), mix_ref[...], preferred_element_type=f32
    ).reshape(UNITS, rows, 4 * points)

    for p in range(RADIX):
        for i in range(blocks):
            zone = zone_ref[(block + i) * RADIX + p]
            base = zone // per_device * (4 * per_device) + zone % per_device
            for r in range(4):
                e_ref[i, r, p : p + 1, :] = jnp.full((1, LANES), table_ref[base + r * per_device], f32)

    def tile(i, l):
        here = pl.ds(i * ZB_R, ZB_R)
        for odd in range(2):
            def load(k):
                start = odd * 2 * points
                re = g_ref[k, here, pl.ds(start + l, LANES)]
                im = g_ref[k, here, pl.ds(start + points + l, LANES)]
                if k == 0:
                    return (re, im)
                row = odd * UNITS + k
                c = cos_ref[row : row + 1, pl.ds(l, LANES)]
                s = sin_ref[row : row + 1, pl.ds(l, LANES)]
                return (re * c - im * s, im * c + re * s)

            pixels = complex_fft([load(k) for k in range(UNITS)], 1)
            for k in range(UNITS):
                p = 2 * k + odd
                re, im = pixels[k]
                power = jnp.maximum(re * re + im * im, DAMPING_FLOOR * DAMPING_FLOOR)
                sine = im * lax.rsqrt(power)
                e = [e_ref[i, r, p : p + 1, :] for r in range(4)]
                height = e[0] + sine * (e[1] + sine * (e[2] + sine * e[3]))
                o_ref[here, pl.ds(p * points + l, LANES)] = height.astype(bf16)

    def group(i, carry):
        for t in range(points // LANES):
            tile(i, t * LANES)
        return carry

    if True:
        lax.fori_loop(0, blocks, group, 0)
    else:
        def one(j, carry):
            tile(j // (points // LANES), pl.multiple_of(j % (points // LANES) * LANES, LANES))
            return carry
        lax.fori_loop(0, blocks * (points // LANES), one, 0)


def row_inverse(field, zones, table, previous, part, shape, per_device, *held):
    part_rows = field.shape[2]
    rows, width = shape
    first = out_part(part, rows)[0]
    block = min(16, part_rows)
    steps = part_rows // block
    start = first // block
    tables = inverse_tables(width)
    smem = pl.BlockSpec(memory_space=pltpu.SMEM)
    extra = [] if previous is None else [previous]
    operands = [zones, table, field, *[jnp.asarray(t) for t in tables], *extra]
    return launch(
        functools.partial(inverse_kernel, first // ZB_R, per_device),
        held,
        operands,
        grid=(steps,),
        in_specs=[smem, smem]
        + [pl.BlockSpec((GROUP, HALVES, block, 2 * LANES), lambda i: (0, 0, i, 0))]
        + [whole(t) for t in tables]
        + [pl.BlockSpec(memory_space=pl.ANY) for _ in extra],
        out_specs=[
            pl.BlockSpec((block, width), lambda i: (start + i, 0)),
            pl.BlockSpec((8, LANES), lambda i: (0, 0)),
        ],
        out_shape=[jax.ShapeDtypeStruct(shape, bf16), jax.ShapeDtypeStruct((8, LANES), f32)],
        scratch_shapes=[
            pltpu.VMEM((UNITS, block, 2 * LANES), bf16),
            pltpu.VMEM((UNITS, block, 4 * width // RADIX), f32),
            pltpu.VMEM((block // ZB_R, 4, RADIX, LANES), f32),
        ],
        aliases={len(operands) - 1: 0} if extra else {},
        name="row_inverse",
        cost=10**12,
    )


def phase_table(rows, devices, offset, period):
    row = jnp.arange(rows, dtype=jnp.int32)[:, None] + offset
    turns = row * jnp.arange(devices, dtype=jnp.int32)[None, :] % period
    angles = turns.astype(f32) * (2.0 * math.pi / period)
    return jnp.cos(angles), jnp.sin(angles)


def body(groups, fringes, lobe_bounds, zone_index, zone_table):
    rows, width = fringes.shape
    devices = groups * GROUP
    height = rows * devices
    every = ("row", "group", "member")
    inside = ("row", "member")
    group = lax.axis_index("group")
    member = lax.axis_index(inside)

    def exchange(block):
        return lax.all_to_all(block, inside, split_axis=0, concat_axis=0, tiled=True)

    per_device = zone_table.shape[1]
    spread = jnp.broadcast_to(zone_table[None], (devices, 4, per_device))
    spread = lax.all_to_all(spread, every, split_axis=0, concat_axis=0, tiled=True)
    table = spread.reshape(-1)
    zones = zone_index.reshape(-1)

    first_offset = 4 * group * rows
    forward_phase = phase_table(rows, devices, first_offset, height)
    inverse_phase = phase_table(rows // 2, devices, first_offset // 2, height // 2)

    part_list = range(ROW_PARTS)
    masks = []
    for h in range(HALVES):
        columns = unit_columns(member + h * GROUP)
        keep = (columns[None, :] >= lobe_bounds[:, :1]) & (columns[None, :] < lobe_bounds[:, 1:])
        keep = keep.astype(f32) * (1.0 / (height * width))
        masks.append(jnp.repeat(jnp.tile(keep, (1, 2)), rows // ROW_PARTS // keep.shape[0], axis=0))

    lobes, late, arrived = [], [], []
    for part in part_list:
        held = [lobes[-1]] if part >= 1 else []
        if part == 1:
            held.append(spread)
        if part >= 2:
            held.append(arrived[part - 2])
        lobe, *late = row_forward(fringes, part, late, *held)
        lobes.append(lobe)
        arrived.append(exchange(lobe))
    firsts = [[], []]
    last = lobes[-1]
    for part in part_list:
        last = column_first(arrived[part], *forward_phase, part, devices, last)
        firsts[0].append(last)
    arrived_late = exchange(gate(late[0], firsts[0][-2]))
    terms = [column_middle(firsts[0], masks[0])]

    def send(pieces):
        return [
            lax.ppermute(pieces[d], "group", [(g, (g + d) % groups) for g in range(groups)])
            for d in range(1, groups)
        ]

    shares = []
    outs = len(OUT_PARTS)

    def finish(index, before, *done):
        h, part = index // outs, index % outs
        held = [before] + [piece for i in done for piece in shares[i][1:]]
        pieces = column_last(terms[h], *inverse_phase, group.reshape(1), part, groups, *held)
        shares.append([pieces[0], *send(pieces)])
        return pieces[0]

    last = finish(0, terms[0])
    last = finish(1, last)
    last = finish(2, last, 0)
    last = finish(3, last, 1)
    last = column_first(arrived_late, *forward_phase, 0, devices, last)
    firsts[1].append(last)
    terms.append(column_middle(firsts[1], masks[1], last))
    last = finish(4, terms[1], 2)
    last = finish(5, last, 3)
    last = finish(6, last, 4)
    last = finish(7, last, 5)

    fields, result = [], None

    def gather(part, before, *done):
        total = add([shares[part], shares[outs + part]], before, *done)
        fields.append(exchange(total))
        return total

    for part in range(2):
        last = gather(part, last)
    for part in range(outs):
        result, last = row_inverse(
            fields[part], zones, table, result, part, (rows // 2, width), per_device, last
        )
        if part + 2 < outs:
            last = gather(part + 2, last, fields[part + 1])
    return result


def solution(mesh):
    row_size, col_size = mesh.shape["row"], mesh.shape["col"]
    groups = row_size * col_size // GROUP
    split = Mesh(
        mesh.devices.reshape(row_size, groups, col_size // groups), ("row", "group", "member")
    )
    every = ("row", "group", "member")
    placed = (P(every, None), P(), P(every, None), P(None, every))
    return jax.shard_map(
        functools.partial(body, groups),
        mesh=split,
        in_specs=placed,
        out_specs=P(every, None),
        check_vma=False,
    )
```

```python
import functools
import math

import jax
import jax.numpy as jnp
import ml_dtypes
import numpy as np
from jax import lax
from jax.experimental import pallas as pl
from jax.experimental.pallas import tpu as pltpu
from jax.sharding import Mesh
from jax.sharding import PartitionSpec as P

ZB_R = 16
LOBE = 4096
LOBE_START = 4096
DAMPING_FLOOR = 0.5

RADIX = 64
UNITS = RADIX // 2
GROUP = 16
HALVES = UNITS // GROUP
LANES = 128
ROW_PARTS = 4
OUT_PARTS = (2, 2, 2, 2)

f32 = jnp.float32
bf16 = jnp.bfloat16
VMEM_LIMIT = 58 * 1024 * 1024


def plus(x, y):
    if x is None:
        return y
    if y is None:
        return x
    return (x[0] + y[0], x[1] + y[1])


def minus(x, y):
    if y is None:
        return x
    if x is None:
        return (-y[0], -y[1])
    return (x[0] - y[0], x[1] - y[1])


def plus_i(x, y, sign):
    if y is None:
        return x
    if x is None:
        return (-y[1], y[0]) if sign > 0 else (y[1], -y[0])
    if sign > 0:
        return (x[0] - y[1], x[1] + y[0])
    return (x[0] + y[1], x[1] - y[0])


def turn(x, num, den):
    num %= den
    if x is None or num == 0:
        return x
    re, im = x
    if 4 * num == den:
        return (-im, re)
    if 2 * num == den:
        return (-re, -im)
    if 4 * num == 3 * den:
        return (im, -re)
    half = math.sqrt(0.5)
    if 8 * num == den:
        return ((re - im) * half, (re + im) * half)
    if 8 * num == 3 * den:
        return ((re + im) * -half, (re - im) * half)
    if 8 * num == 5 * den:
        return ((im - re) * half, (re + im) * -half)
    if 8 * num == 7 * den:
        return ((re + im) * half, (im - re) * half)
    c = math.cos(2 * math.pi * num / den)
    s = math.sin(2 * math.pi * num / den)
    return (re * c - im * s, im * c + re * s)


def complex_fft(xs, sign):
    n = len(xs)
    if n == 1:
        return list(xs)
    if n == 2:
        return [plus(xs[0], xs[1]), minus(xs[0], xs[1])]
    even = complex_fft(xs[0::2], sign)
    one = complex_fft(xs[1::4], sign)
    three = complex_fft(xs[3::4], sign)
    out = [None] * n
    for k in range(n // 4):
        t1 = turn(one[k], sign * k, n)
        t3 = turn(three[k], sign * 3 * k, n)
        total, diff = plus(t1, t3), minus(t1, t3)
        out[k] = plus(even[k], total)
        out[k + n // 2] = minus(even[k], total)
        out[k + n // 4] = plus_i(even[k + n // 4], diff, sign)
        out[k + 3 * n // 4] = plus_i(even[k + n // 4], diff, -sign)
    return out


def real_fft(xs):
    n = len(xs)
    if n == 1:
        return [(xs[0], None)]
    if n == 2:
        return [(xs[0] + xs[1], None), (xs[0] - xs[1], None)]
    even = real_fft(xs[0::2])
    one = real_fft(xs[1::4])
    three = real_fft(xs[3::4])
    out = [None] * (n // 2 + 1)
    total, diff = one[0][0] + three[0][0], one[0][0] - three[0][0]
    out[0] = (even[0][0] + total, None)
    out[n // 2] = (even[0][0] - total, None)
    out[n // 4] = (even[n // 4][0], -diff)
    for k in range(1, n // 8 + 1):
        if one[k][1] is None:
            c1, s1 = math.cos(2 * math.pi * k / n), math.sin(2 * math.pi * k / n)
            c3, s3 = math.cos(6 * math.pi * k / n), math.sin(6 * math.pi * k / n)
            t1 = (one[k][0] * c1, one[k][0] * -s1)
            t3 = (three[k][0] * c3, three[k][0] * -s3)
        else:
            t1 = turn(one[k], -k, n)
            t3 = turn(three[k], -3 * k, n)
        total, diff = plus(t1, t3), minus(t1, t3)
        low, high = even[k], even[n // 4 - k]
        if low[1] is None:
            out[k] = (low[0] + total[0], total[1])
            out[n // 2 - k] = (low[0] - total[0], total[1])
        else:
            out[k] = (low[0] + total[0], low[1] + total[1])
            out[n // 2 - k] = (low[0] - total[0], total[1] - low[1])
        if k != n // 4 - k:
            if high[1] is None:
                out[n // 4 + k] = (high[0] + diff[1], -diff[0])
                out[n // 4 - k] = (high[0] - diff[1], -diff[0])
            else:
                out[n // 4 + k] = (high[0] + diff[1], -(high[1] + diff[0]))
                out[n // 4 - k] = (high[0] - diff[1], high[1] - diff[0])
    return out


def cos_sin(turns, period):
    angles = (turns % period) * (2.0 * np.pi / period)
    return np.cos(angles), np.sin(angles)


def as_bf16(table):
    return table.astype(np.float32).astype(ml_dtypes.bfloat16)


def forward_tables(width):
    points = width // RADIX
    per_residue = LOBE // RADIX
    b = np.arange(points)[:, None]
    twist_cos, twist_sin = cos_sin(np.arange(UNITS + 1)[:, None] * b.T, width)
    j = LOBE_START // RADIX + np.arange(per_residue)[None, :]
    c1, s1 = cos_sin(b * j, points)
    c2, s2 = cos_sin(b * (j + 1), points)
    mix = np.block([[c1, c2, -s1, -s2], [s1, -s2, c1, -c2]])
    return twist_cos.astype(np.float32), twist_sin.astype(np.float32), as_bf16(mix)


def inverse_tables(width):
    points = width // RADIX
    per_residue = LOBE // RADIX
    q = np.arange(points)[None, :]
    residue = np.arange(UNITS)[:, None]
    turns = np.concatenate([residue * q, residue * (q + points)])
    twist_cos, twist_sin = cos_sin(turns, width)
    column = np.arange(per_residue)[:, None]
    c1, s1 = cos_sin(column * q, points)
    c2, s2 = cos_sin((2 * column + 1) * q, 2 * points)
    mix = np.block([[c1, s1, c1, s1], [c2, s2, -c2, -s2], [-s1, c1, -s1, c1], [-s2, c2, s2, -c2]])
    return twist_cos.astype(np.float32), twist_sin.astype(np.float32), as_bf16(mix)


def column_tables(rows):
    part = rows // ROW_PARTS
    b = np.arange(part)[None, :]
    m = np.arange(part)[:, None]
    forward = []
    for q in range(ROW_PARTS):
        c, s = cos_sin(b * (q + ROW_PARTS * m), rows)
        forward.append(np.concatenate([c, s], axis=1))
    out_row = np.arange(rows // 2)[:, None]
    order = (np.arange(ROW_PARTS)[:, None] + ROW_PARTS * np.arange(part // 2)[None, :]).reshape(1, -1)
    c, s = cos_sin(out_row * order, rows // 2)
    return as_bf16(np.stack(forward)), as_bf16(np.concatenate([c, s], axis=1))


def out_part(part, rows):
    eighth = rows // 8
    return sum(OUT_PARTS[:part]) * eighth, OUT_PARTS[part] * eighth


def unit_columns(unit):
    lane = jnp.arange(LANES, dtype=jnp.int32)
    per_residue = LOBE // RADIX
    second = jnp.where(unit == 0, RADIX // 2, RADIX - unit)
    return RADIX * (lane % per_residue) + jnp.where(lane < per_residue, unit, second)


def launch(kernel, held, operands, in_specs, aliases=None, cost=1, **options):
    count = len(held)
    return pl.pallas_call(
        lambda *refs: kernel(*refs[count:]),
        in_specs=[pl.BlockSpec(memory_space=pl.ANY)] * count + in_specs,
        input_output_aliases={count + k: v for k, v in (aliases or {}).items()},
        compiler_params=pltpu.CompilerParams(vmem_limit_bytes=VMEM_LIMIT),
        cost_estimate=pl.CostEstimate(flops=cost, bytes_accessed=cost, transcendentals=0),
        **options,
    )(*held, *operands)


def gate(value, *held):
    spec = pl.BlockSpec(memory_space=pl.ANY)
    return launch(
        lambda *refs: None,
        held,
        [value],
        in_specs=[spec],
        out_specs=spec,
        out_shape=jax.ShapeDtypeStruct(value.shape, value.dtype),
        aliases={0: 0},
        name="gate",
    )


def whole(array):
    return pl.BlockSpec(array.shape, lambda *_: (0,) * array.ndim)


def forward_kernel(x_ref, cos_ref, sin_ref, mix_ref, *refs):
    outs, slots = refs[:HALVES], refs[HALVES:]
    rows, width = x_ref.shape
    points = width // RADIX
    tiles = points // LANES
    lane = lax.broadcasted_iota(jnp.int32, (16, 2 * LANES), 1)
    first_residue = lane % LANES < LANES // 2

    def butterfly(z_ref, r, l):
        here = pl.ds(r, 16)
        xs = [x_ref[here, pl.ds(a * points + l, LANES)].astype(f32) for a in range(RADIX)]
        spectrum = real_fft(xs)
        z_ref[0, :, pl.ds(l, LANES)] = spectrum[0][0].astype(bf16)
        z_ref[0, :, pl.ds(points + l, LANES)] = jnp.zeros((16, LANES), bf16)
        for k in range(1, UNITS + 1):
            re, im = spectrum[k]
            c = cos_ref[k : k + 1, pl.ds(l, LANES)]
            s = sin_ref[k : k + 1, pl.ds(l, LANES)]
            if im is None:
                z_ref[k, :, pl.ds(l, LANES)] = (re * c).astype(bf16)
                z_ref[k, :, pl.ds(points + l, LANES)] = (re * -s).astype(bf16)
            else:
                z_ref[k, :, pl.ds(l, LANES)] = (re * c + im * s).astype(bf16)
                z_ref[k, :, pl.ds(points + l, LANES)] = (im * c - re * s).astype(bf16)

    def mix(z_ref, r):
        z = z_ref[...].reshape((UNITS + 1) * 16, 2 * points)
        lobe = jnp.dot(z, mix_ref[...], preferred_element_type=f32)
        lobe = lobe.astype(bf16).reshape(UNITS + 1, 16, 2 * LANES)
        here = pl.ds(r, 16)
        outs[0][0, here] = jnp.where(first_residue, lobe[0], lobe[UNITS])
        outs[0][1:, here] = lobe[1:GROUP]
        for h in range(1, HALVES):
            outs[h][:, here] = lobe[h * GROUP : (h + 1) * GROUP]

    for g in range(rows // 16):
        for t in range(tiles):
            butterfly(slots[0], g * 16, t * LANES)
        mix(slots[0], g * 16)


def row_forward(fringes, part, late, *held):
    rows, width = fringes.shape
    part_rows = rows // ROW_PARTS
    block = min(16, part_rows)
    steps = part_rows // block
    tables = forward_tables(width)
    operands = [fringes, *[jnp.asarray(t) for t in tables], *late]
    count = len(operands) - len(late)
    return launch(
        lambda *refs: forward_kernel(*refs[:count], *refs[count + len(late) :]),
        held,
        operands,
        grid=(steps,),
        in_specs=[pl.BlockSpec((block, width), lambda i: (part * steps + i, 0))]
        + [whole(t) for t in tables]
        + [pl.BlockSpec(memory_space=pl.ANY) for _ in late],
        out_specs=[
            pl.BlockSpec((GROUP, block, 2 * LANES), lambda i: (0, i, 0)),
            pl.BlockSpec((GROUP, block, 2 * LANES), lambda i: (0, part * steps + i, 0)),
        ],
        out_shape=[
            jax.ShapeDtypeStruct((GROUP, part_rows, 2 * LANES), bf16),
            jax.ShapeDtypeStruct((GROUP, rows, 2 * LANES), bf16),
        ],
        aliases={count: 1} if late else {},
        scratch_shapes=[pltpu.VMEM((UNITS + 1, 16, 2 * width // RADIX), bf16)] * 2,
        name="row_forward",
    )


def first_kernel(devices, x_ref, cos_ref, sin_ref, o_ref):
    rows = x_ref.shape[1]

    def step(i, carry):
        here = pl.ds(pl.multiple_of(i * 16, 16), 16)
        cos_tab = cos_ref[here, :]
        sin_tab = sin_ref[here, :]

        def load(e):
            return (x_ref[e, here, :LANES].astype(f32), x_ref[e, here, LANES:].astype(f32))

        coarse = [complex_fft([load(rho * 4 + gamma) for rho in range(4)], -1) for gamma in range(4)]
        for q in range(4):
            fine = [turn(coarse[gamma][q], -gamma * q, devices) for gamma in range(4)]
            fine = complex_fft(fine + [None] * (devices // 4 - 4), -1)
            for p in range(devices // 4):
                u = q + 4 * p
                re, im = fine[p]
                c = cos_tab[:, u : u + 1]
                s = sin_tab[:, u : u + 1]
                o_ref[u, here, :LANES] = (re * c + im * s).astype(bf16)
                o_ref[u, here, LANES:] = (im * c - re * s).astype(bf16)
        return carry

    lax.fori_loop(0, rows // 16, step, 0)


def column_first(received, cos_tab, sin_tab, part, devices, *held):
    total, rows = cos_tab.shape[0], received.shape[1]
    block = min(64, total // ROW_PARTS)
    steps = rows // block
    start = 0 if rows == total else part * steps
    table = pl.BlockSpec((block, devices), lambda i: (start + i, 0))
    return launch(
        functools.partial(first_kernel, devices),
        held,
        [received, cos_tab, sin_tab],
        grid=(steps,),
        in_specs=[pl.BlockSpec((GROUP, block, 2 * LANES), lambda i: (0, i, 0)), table, table],
        out_specs=pl.BlockSpec((devices, block, 2 * LANES), lambda i: (0, i, 0)),
        out_shape=jax.ShapeDtypeStruct((devices, rows, 2 * LANES), bf16),
        name="column_first",
    )


def middle_kernel(*refs):
    parts, (forward_ref, inverse_ref, mask_ref, o_ref) = refs[:ROW_PARTS], refs[ROW_PARTS:]
    count = parts[0].shape[1]
    for u in range(o_ref.shape[0]):
        xs = [(ref[u, :, :LANES].astype(f32), ref[u, :, LANES:].astype(f32)) for ref in parts]
        mixed = complex_fft(xs, -1)
        folded_re, folded_im = [], []
        for q in range(ROW_PARTS):
            re, im = mixed[q][0].astype(bf16), mixed[q][1].astype(bf16)
            data = jnp.concatenate(
                [jnp.concatenate([re, im], axis=1), jnp.concatenate([im, -re], axis=1)], axis=0
            )
            spectrum = jnp.dot(forward_ref[q], data, preferred_element_type=f32) * mask_ref[...]
            folded = (spectrum[: count // 2] + spectrum[count // 2 :]).astype(bf16)
            folded_re.append(folded[:, :LANES])
            folded_im.append(folded[:, LANES:])
        re = jnp.concatenate(folded_re, axis=0)
        im = jnp.concatenate(folded_im, axis=0)
        data = jnp.concatenate(
            [jnp.concatenate([re, im], axis=1), jnp.concatenate([-im, re], axis=1)], axis=0
        )
        o_ref[u] = jnp.dot(inverse_ref[...], data, preferred_element_type=f32).astype(bf16)


def column_middle(parts, mask, *held):
    devices = parts[0].shape[0]
    rows = sum(part.shape[1] for part in parts)
    part_rows = rows // ROW_PARTS
    block = 4
    tables = column_tables(rows)
    if len(parts) == 1:
        parts = parts * ROW_PARTS
        places = range(ROW_PARTS)
    else:
        places = [0] * ROW_PARTS
    pieces = [pl.BlockSpec((block, part_rows, 2 * LANES), lambda u, r=r: (u, r, 0)) for r in places]
    return launch(
        middle_kernel,
        held,
        [*parts, *[jnp.asarray(t) for t in tables], mask],
        grid=(devices // block,),
        in_specs=pieces + [whole(t) for t in tables] + [whole(mask)],
        out_specs=pl.BlockSpec((block, rows // 2, 2 * LANES), lambda u: (u, 0, 0)),
        out_shape=jax.ShapeDtypeStruct((devices, rows // 2, 2 * LANES), bf16),
        name="column_middle",
    )


def last_kernel(devices, groups, group_ref, x_ref, cos_ref, sin_ref, *outs):
    rows = x_ref.shape[1]
    columns = devices // 4

    def step(i, carry):
        here = pl.ds(pl.multiple_of(i * 16, 16), 16)
        cos_tab = cos_ref[here, :]
        sin_tab = sin_ref[here, :]
        xs = []
        for u in range(devices):
            re = x_ref[u, here, :LANES].astype(f32)
            im = x_ref[u, here, LANES:].astype(f32)
            c = cos_tab[:, u : u + 1]
            s = sin_tab[:, u : u + 1]
            xs.append((re * c - im * s, im * c + re * s))
        ys = complex_fft(xs, 1)
        for delta in range(groups):
            carry_over = (group_ref[0] + delta) // groups
            for rho in range(4):
                for gamma in range(4):
                    re, im = ys[columns * rho + 4 * delta + gamma]
                    e = (rho + carry_over) % 4 * 4 + gamma if delta else rho * 4 + gamma
                    outs[delta][e, here, :LANES] = re.astype(bf16)
                    outs[delta][e, here, LANES:] = im.astype(bf16)
        return carry

    lax.fori_loop(0, rows // 16, step, 0)


def column_last(terms, cos_tab, sin_tab, group, part, groups, *held):
    devices, total, _ = terms.shape
    first, rows = out_part(part, total)
    block = math.gcd(first, rows, 64)
    steps = rows // block
    start = first // block
    table = pl.BlockSpec((block, devices), lambda i: (start + i, 0))
    return launch(
        functools.partial(last_kernel, devices, groups),
        held,
        [group, terms, cos_tab, sin_tab],
        grid=(steps,),
        in_specs=[
            pl.BlockSpec(memory_space=pltpu.SMEM),
            pl.BlockSpec((devices, block, 2 * LANES), lambda i: (0, start + i, 0)),
            table,
            table,
        ],
        out_specs=[pl.BlockSpec((GROUP, block, 2 * LANES), lambda i: (0, i, 0))] * groups,
        out_shape=[jax.ShapeDtypeStruct((GROUP, rows, 2 * LANES), bf16)] * groups,
        name="column_last",
    )


def sum_kernel(*refs):
    o_ref = refs[-1]
    count = len(refs) // HALVES
    for h in range(HALVES):
        total = refs[h * count][...].astype(f32)
        for ref in refs[h * count + 1 : (h + 1) * count]:
            total = total + ref[...].astype(f32)
        o_ref[:, h] = total.astype(bf16)


def add(pieces, cost, *held):
    operands = [piece for shares in pieces for piece in shares]
    members, rows, lanes = operands[0].shape
    block = 4
    return launch(
        sum_kernel,
        held,
        operands,
        grid=(members // block,),
        in_specs=[pl.BlockSpec((block, rows, lanes), lambda i: (i, 0, 0))] * len(operands),
        out_specs=pl.BlockSpec((block, HALVES, rows, lanes), lambda i: (i, 0, 0, 0)),
        out_shape=jax.ShapeDtypeStruct((members, HALVES, rows, lanes), bf16),
        name="sum_shares",
        cost=cost,
    )


def inverse_kernel(first_block, per_device, zone_ref, table_ref, field_ref, *refs):
    cos_ref, sin_ref, mix_ref = refs[:3]
    o_ref, token_ref, f_ref, g_ref, e_ref = refs[-5:]
    token_ref[...] = jnp.zeros_like(token_ref)
    rows, width = o_ref.shape
    points = width // RADIX
    blocks = rows // ZB_R
    block = first_block + pl.program_id(0) * blocks
    lane = lax.broadcasted_iota(jnp.int32, (rows, 2 * LANES), 1)
    first_residue = lane % LANES < LANES // 2

    def unit(u):
        return field_ref[u % GROUP, u // GROUP]

    for k in range(UNITS):
        f_ref[k] = jnp.where(first_residue, unit(k), unit(-k % UNITS))
    g_ref[...] = jnp.dot(
        f_ref[...].reshape(UNITS * rows, 2 * LANES), mix_ref[...], preferred_element_type=f32
    ).reshape(UNITS, rows, 4 * points)

    for p in range(RADIX):
        for i in range(blocks):
            zone = zone_ref[(block + i) * RADIX + p]
            base = zone // per_device * (4 * per_device) + zone % per_device
            for r in range(4):
                e_ref[i, r, p : p + 1, :] = jnp.full((1, LANES), table_ref[base + r * per_device], f32)

    def tile(i, l):
        here = pl.ds(i * ZB_R, ZB_R)
        for odd in range(2):
            def load(k):
                start = odd * 2 * points
                re = g_ref[k, here, pl.ds(start + l, LANES)]
                im = g_ref[k, here, pl.ds(start + points + l, LANES)]
                if k == 0:
                    return (re, im)
                row = odd * UNITS + k
                c = cos_ref[row : row + 1, pl.ds(l, LANES)]
                s = sin_ref[row : row + 1, pl.ds(l, LANES)]
                return (re * c - im * s, im * c + re * s)

            pixels = complex_fft([load(k) for k in range(UNITS)], 1)
            for k in range(UNITS):
                p = 2 * k + odd
                re, im = pixels[k]
                power = jnp.maximum(re * re + im * im, DAMPING_FLOOR * DAMPING_FLOOR)
                sine = im * lax.rsqrt(power)
                e = [e_ref[i, r, p : p + 1, :] for r in range(4)]
                height = e[0] + sine * (e[1] + sine * (e[2] + sine * e[3]))
                o_ref[here, pl.ds(p * points + l, LANES)] = height.astype(bf16)

    def group(i, carry):
        for t in range(points // LANES):
            tile(i, t * LANES)
        return carry

    lax.fori_loop(0, blocks, group, 0)


def row_inverse(field, zones, table, previous, part, shape, per_device, *held):
    part_rows = field.shape[2]
    rows, width = shape
    first = out_part(part, rows)[0]
    block = min(16, part_rows)
    steps = part_rows // block
    start = first // block
    tables = inverse_tables(width)
    smem = pl.BlockSpec(memory_space=pltpu.SMEM)
    extra = [] if previous is None else [previous]
    operands = [zones, table, field, *[jnp.asarray(t) for t in tables], *extra]
    return launch(
        functools.partial(inverse_kernel, first // ZB_R, per_device),
        held,
        operands,
        grid=(steps,),
        in_specs=[smem, smem]
        + [pl.BlockSpec((GROUP, HALVES, block, 2 * LANES), lambda i: (0, 0, i, 0))]
        + [whole(t) for t in tables]
        + [pl.BlockSpec(memory_space=pl.ANY) for _ in extra],
        out_specs=[
            pl.BlockSpec((block, width), lambda i: (start + i, 0)),
            pl.BlockSpec((8, LANES), lambda i: (0, 0)),
        ],
        out_shape=[jax.ShapeDtypeStruct(shape, bf16), jax.ShapeDtypeStruct((8, LANES), f32)],
        scratch_shapes=[
            pltpu.VMEM((UNITS, block, 2 * LANES), bf16),
            pltpu.VMEM((UNITS, block, 4 * width // RADIX), f32),
            pltpu.VMEM((block // ZB_R, 4, RADIX, LANES), f32),
        ],
        aliases={len(operands) - 1: 0} if extra else {},
        name="row_inverse",
        cost=10**12,
    )


def phase_table(rows, devices, offset, period):
    row = jnp.arange(rows, dtype=jnp.int32)[:, None] + offset
    turns = row * jnp.arange(devices, dtype=jnp.int32)[None, :] % period
    angles = turns.astype(f32) * (2.0 * math.pi / period)
    return jnp.cos(angles), jnp.sin(angles)


def body(groups, fringes, lobe_bounds, zone_index, zone_table):
    rows, width = fringes.shape
    devices = groups * GROUP
    height = rows * devices
    every = ("row", "group", "member")
    inside = ("row", "member")
    group = lax.axis_index("group")
    member = lax.axis_index(inside)

    def exchange(block):
        return lax.all_to_all(block, inside, split_axis=0, concat_axis=0, tiled=True)

    per_device = zone_table.shape[1]
    spread = jnp.broadcast_to(zone_table[None], (devices, 4, per_device))
    spread = lax.all_to_all(spread, every, split_axis=0, concat_axis=0, tiled=True)
    table = spread.reshape(-1)
    zones = zone_index.reshape(-1)

    first_offset = 4 * group * rows
    forward_phase = phase_table(rows, devices, first_offset, height)
    inverse_phase = phase_table(rows // 2, devices, first_offset // 2, height // 2)

    part_list = range(ROW_PARTS)
    masks = []
    for h in range(HALVES):
        columns = unit_columns(member + h * GROUP)
        keep = (columns[None, :] >= lobe_bounds[:, :1]) & (columns[None, :] < lobe_bounds[:, 1:])
        keep = keep.astype(f32) * (1.0 / (height * width))
        masks.append(jnp.repeat(jnp.tile(keep, (1, 2)), rows // ROW_PARTS // keep.shape[0], axis=0))

    lobes, late, arrived = [], [], []
    for part in part_list:
        held = [lobes[-1]] if part >= 1 else []
        if part == 1:
            held.append(spread)
        if part >= 2:
            held.append(arrived[part - 2])
        lobe, *late = row_forward(fringes, part, late, *held)
        lobes.append(lobe)
        arrived.append(exchange(lobe))
    firsts = [[], []]
    last = lobes[-1]
    for part in part_list:
        last = column_first(arrived[part], *forward_phase, part, devices, last)
        firsts[0].append(last)
    arrived_late = exchange(gate(late[0], firsts[0][-2]))
    terms = [column_middle(firsts[0], masks[0])]

    def send(pieces):
        return [
            lax.ppermute(pieces[d], "group", [(g, (g + d) % groups) for g in range(groups)])
            for d in range(1, groups)
        ]

    shares = []
    outs = len(OUT_PARTS)

    def finish(index, before, *done):
        h, part = index // outs, index % outs
        held = [before] + [piece for i in done for piece in shares[i][1:]]
        pieces = column_last(terms[h], *inverse_phase, group.reshape(1), part, groups, *held)
        shares.append([pieces[0], *send(pieces)])
        return pieces[0]

    last = finish(0, terms[0])
    last = finish(1, last)
    last = finish(2, last, 0)
    last = finish(3, last, 1)
    last = column_first(arrived_late, *forward_phase, 0, devices, last)
    firsts[1].append(last)
    terms.append(column_middle(firsts[1], masks[1], last))
    last = finish(4, terms[1], 2)
    last = finish(5, last, 3)

    fields, result = [], None

    def gather(part, before, *done):
        total = add([shares[part], shares[outs + part]], 10**12 if part == 1 else 1, before, *done)
        fields.append(exchange(total))
        return total

    last = finish(6, last, 4)
    last = finish(7, last)
    last = gather(0, last)
    last = gather(1, last)
    for part in range(outs):
        result, last = row_inverse(
            fields[part], zones, table, result, part, (rows // 2, width), per_device, last
        )
        if part + 2 < outs:
            last = gather(part + 2, last, fields[part + 1])
    return result


def solution(mesh):
    row_size, col_size = mesh.shape["row"], mesh.shape["col"]
    groups = row_size * col_size // GROUP
    split = Mesh(
        mesh.devices.reshape(row_size, groups, col_size // groups), ("row", "group", "member")
    )
    every = ("row", "group", "member")
    placed = (P(every, None), P(), P(every, None), P(None, every))
    return jax.shard_map(
        functools.partial(body, groups),
        mesh=split,
        in_specs=placed,
        out_specs=P(every, None),
        check_vma=False,
    )
```
